128 devices in a mesh: kvp: 16 (over z, x), tp: 8 (over y, core).
Axes of the slice: x: 4, y: 4, z: 4, core: 2. Of those that a mesh axis runs over, the one named last changes fastest.
Arguments:
- queries: bfloat16 [4, 128, 4, 128], P(None, 'tp'), may hold values from -128 to 128
- key_cache_rows: bfloat16 [4, 8, 16384, 128], P(None, 'tp', 'kvp'), may hold values from -6 to 6
- value_cache_rows: bfloat16 [4, 8, 16384, 128], P(None, 'tp', 'kvp'), may hold values from -6 to 6
- k_new: bfloat16 [4, 8, 4, 128], P(None, 'tp'), may hold values from -4 to 4
- v_new: bfloat16 [4, 8, 4, 128], P(None, 'tp'), may hold values from -6 to 6
- lengths: int32 [4], replicated, may hold values from 1 to 16365, as said below
- new_owner: int32 [4], replicated, may hold values from 0 to 15, as said below
- residual: bfloat16 [4, 4, 16384], P(None, None, 'kvp'), may hold values from -10 to 10
- norm_gain: float32 [16384], P('kvp'), may hold values from 0.1 to 1.9
- out_weight: bfloat16 [8, 16, 128, 16384], P('tp', 'kvp'), may hold values from -0.0625 to 0.0625
- gate_weight: bfloat16 [16384, 26624], P('kvp', 'tp'), may hold values from -0.046875 to 0.046875
- up_weight: bfloat16 [16384, 26624], P('kvp', 'tp'), may hold values from -0.046875 to 0.046875
- down_weight: bfloat16 [26624, 16384], P('tp', 'kvp'), may hold values from -0.0390625 to 0.0390625
Outputs:
- attended: bfloat16 [4, 8, 16, 4, 128], P(None, 'tp', 'kvp')
- stream_mid: bfloat16 [4, 4, 16384], P(None, None, 'kvp')
- layer_out: bfloat16 [4, 4, 16384], P(None, None, 'kvp')
The draws below stay inside these ranges and needn't reach their ends.
Inputs may be any that keep to these rules, and one draw needn't show every extreme that they name: `lengths`: some sequence has exactly 16365 cached tokens. `new_owner`: the first two sequences have different owners.
All inputs are finite; a program needn't handle non-finite values.
Results may differ from the reference program's by a relative error of at most 0.011.
Values sent between devices are 32-bit elements; how exact they have to be, the bound alone decides.
No kernel may reach another device: no remote copies, remote signals or barrier semaphores. Data moves between devices by JAX's collectives and lax.ppermute only.
A program may use at most 128 MiB of HBM per device.

```python
import math
import jax
import jax.numpy as jnp
from jax import lax

D = 16384
HQ = 128
KVH = 8
HD = 128
FFW = 26624
SEQS = 4
SLOTS = 1024
DRAFT = 4
GROUP = 16
CTX = 16384
MAXLEN = 16365
N_KVP = 16


def common_keys(key):
    return jnp.clip(jax.random.normal(key, (SEQS, KVH, DRAFT, HD), jnp.float32), -4.0, 4.0)


def draw_k_new(key, part):
    base = common_keys(key)
    return base.astype(jnp.bfloat16)


def draw_queries(key, part):
    key = jax.random.fold_in(key, 7)
    base = jnp.clip(2.5 * jax.random.normal(key, (SEQS, HQ, DRAFT, HD), jnp.float32), -15.0, 15.0)
    return base.astype(jnp.bfloat16)


def draw_lengths(key, part):
    key = jax.random.fold_in(key, 3)
    values = jax.random.randint(key, (SEQS,), 1, MAXLEN + 1, dtype=jnp.int32)
    chosen = jax.random.randint(jax.random.fold_in(key, 5), (), 0, SEQS, dtype=jnp.int32)
    return values.at[chosen].set(MAXLEN)


def draw_new_owner(key, part):
    key = jax.random.fold_in(key, 11)
    jump = jax.random.randint(key, (), 1, N_KVP, dtype=jnp.int32)
    index = jnp.arange(SEQS, dtype=jnp.int32)
    return (N_KVP - 1 - index * jump) % N_KVP


def draw_residual(key, part):
    key = jax.random.fold_in(key, 13)
    place = jnp.arange(D, dtype=jnp.float32) / (D - 1)
    scale = 0.25 * jnp.exp(math.log(8.0) * place)
    base = jnp.clip(jax.random.normal(key, (SEQS, DRAFT, D), jnp.float32), -5.0, 5.0)
    return (base * scale).astype(jnp.bfloat16)


def strengthened(drawn, key, source, target, blocks, factor):
    owner, partner = [(jnp.arange(drawn.shape[dim]) // (drawn.shape[dim] // blocks)).reshape([-1 if axis == dim else 1 for axis in range(drawn.ndim)]) for dim in (source, target)]
    chosen = jax.random.permutation(key, blocks)[partner]
    strong = (owner == chosen) | (owner == (partner + blocks // 2) % blocks)
    return jnp.where(strong, factor * drawn, drawn)


def level_of(rng, extent, cuts, smallest, high):
    gain, own = 1.0, jax.random.fold_in(rng, 6)
    for dim, parts in cuts:
        heights = jnp.exp(jax.random.uniform(jax.random.fold_in(own, dim), (parts,), jnp.float32, smallest / len(cuts), high / len(cuts)))
        gain = gain * jnp.repeat(heights, extent[dim] // parts).reshape([-1 if axis == dim else 1 for axis in range(len(extent))])
    return gain


def normal_values(stream_key, extent, spread, bound, cuts=(), kind=jnp.bfloat16):
    factor_of = level_of(stream_key, extent, cuts, -0.22, 0.18) if cuts else 1.0
    drawn = jax.random.normal(stream_key, extent, jnp.float32) * spread * factor_of
    return jnp.minimum(jnp.maximum(drawn, -bound), bound).astype(kind)


def bell_draw_with(key, dims, scale, bound, split, heavy, kind=jnp.bfloat16):
    entries = scale * jax.random.normal(key, dims, jnp.float32)
    if split:
        entries = entries * level_of(key, dims, split, -0.22, 0.18)
    return jnp.clip(strengthened(entries, jax.random.fold_in(key, 3), *heavy), -bound, bound).astype(kind)


def setup_inputs(seed: int = 0) -> dict:
    splits = jax.random.split(jax.random.key(seed), 14)
    return {
        "queries": draw_queries(jax.random.fold_in(splits[13], 71), 0),
        "key_cache_rows": normal_values(splits[1], (SEQS, KVH, CTX, HD), 1.0, 6.0, ((1, 8), (2, 16))),
        "value_cache_rows": normal_values(splits[2], (SEQS, KVH, CTX, HD), 1.0, 6.0, ((1, 8), (2, 16))),
        "k_new": draw_k_new(jax.random.fold_in(splits[13], 71), 0),
        "v_new": normal_values(splits[4], (SEQS, KVH, DRAFT, HD), 1.0, 6.0, ((1, 8),)),
        "lengths": draw_lengths(jax.random.fold_in(splits[13], 71), 0),
        "new_owner": draw_new_owner(jax.random.fold_in(splits[13], 71), 0),
        "residual": draw_residual(jax.random.fold_in(splits[13], 71), 0),
        "norm_gain": jnp.clip(1.0 + 0.18 * jax.random.normal(splits[8], (D,), jnp.float32), 0.1, 1.9),
        "out_weight": bell_draw_with(splits[9], (KVH, GROUP, HD, D), (HQ * HD) ** -0.5, 0.0625, ((0, 8), (1, 16)), (1, 3, 16, 2.0)),
        "gate_weight": normal_values(splits[10], (D, FFW), D ** -0.5, 0.046875, ((0, 16), (1, 8))),
        "up_weight": normal_values(splits[11], (D, FFW), D ** -0.5, 0.046875, ((0, 16), (1, 8))),
        "down_weight": normal_values(splits[12], (FFW, D), FFW ** -0.5, 0.0390625, ((0, 8), (1, 16))),
    }


def attend_one(pieces):
    queries, key_cache_rows, value_cache_rows, k_new, v_new, length, owner_idx = pieces
    position = jnp.arange(CTX, dtype=jnp.int32)
    device_of = position // SLOTS
    linear = position % SLOTS * N_KVP + device_of
    offset = (owner_idx - length) % N_KVP
    token_pos = linear - offset
    live_mask = (token_pos >= 0) & (token_pos < length)
    scale_factor_term = 1.0 / math.sqrt(HD)
    grouped_query_rows = queries.reshape(KVH, GROUP * DRAFT, HD).astype(jnp.float32)
    logit_scores = jnp.einsum('spy,sly->spl', grouped_query_rows, key_cache_rows.astype(jnp.float32)) * scale_factor_term
    fresh_scores = jnp.einsum('grd,gid->gri', grouped_query_rows, k_new.astype(jnp.float32)) * scale_factor_term
    row_draft = jnp.arange(GROUP * DRAFT, dtype=jnp.int32) % DRAFT
    causal = jnp.arange(DRAFT, dtype=jnp.int32)[None, :] <= row_draft[:, None]
    logit_scores = jnp.where(live_mask[None, None, :], logit_scores, -1e+30)
    fresh_scores = jnp.where(causal[None], fresh_scores, -1e+30)
    row_top = jnp.maximum(lax.optimization_barrier(jnp.max(logit_scores, axis=-1)), lax.optimization_barrier(jnp.max(fresh_scores, axis=-1)))
    weights = jnp.where(live_mask[None, None, :], jnp.exp(logit_scores - row_top[..., None]), 0.0)
    fresh_weights = jnp.where(causal[None], jnp.exp(fresh_scores - row_top[..., None]), 0.0)
    row_total = lax.optimization_barrier(jnp.sum(weights, axis=-1)) + lax.optimization_barrier(jnp.sum(fresh_weights, axis=-1))
    rounded_values = lax.optimization_barrier(weights.astype(jnp.bfloat16)).astype(jnp.float32)
    fresh_rounded = lax.optimization_barrier(fresh_weights.astype(jnp.bfloat16)).astype(jnp.float32)
    weighted_values = jnp.einsum('vow,vwx->vox', rounded_values, value_cache_rows.astype(jnp.float32))
    weighted_values = weighted_values + jnp.einsum('gri,gid->grd', fresh_rounded, v_new.astype(jnp.float32))
    result = weighted_values / row_total[..., None]
    return result.reshape(KVH, GROUP, DRAFT, HD).astype(jnp.bfloat16)

def reference(queries, key_cache_rows, value_cache_rows, k_new, v_new, lengths, new_owner, residual, norm_gain, out_weight, gate_weight, up_weight, down_weight):
    attended = lax.map(attend_one, (queries, key_cache_rows, value_cache_rows, k_new, v_new, lengths, new_owner))
    row_count = SEQS * DRAFT
    flat_rows = attended.transpose(0, 3, 1, 2, 4).reshape(row_count, HQ * HD)
    projected = jnp.dot(flat_rows, out_weight.reshape(HQ * HD, D), preferred_element_type=jnp.float32)
    stream_mid = (residual.reshape(row_count, D).astype(jnp.float32) + projected).astype(jnp.bfloat16)
    wide = stream_mid.astype(jnp.float32)
    mean_square = lax.optimization_barrier(jnp.mean(wide * wide, axis=-1, keepdims=True))
    normed = (wide * lax.rsqrt(mean_square + 1e-05) * norm_gain).astype(jnp.bfloat16)
    gate = jnp.dot(normed, gate_weight, preferred_element_type=jnp.float32)
    upper = jnp.dot(normed, up_weight, preferred_element_type=jnp.float32)
    active = (jax.nn.silu(gate) * upper).astype(jnp.bfloat16)
    lowered = jnp.dot(active, down_weight, preferred_element_type=jnp.float32)
    layer_out = (wide + lowered).astype(jnp.bfloat16)
    return (attended, stream_mid.reshape(SEQS, DRAFT, D), layer_out.reshape(SEQS, DRAFT, D))
```

```python
import math

import jax
import jax.numpy as jnp
from jax import lax
from jax.experimental import pallas as pl
from jax.experimental.pallas import tpu as pltpu
from jax.sharding import PartitionSpec as P

D = 16384
KVP = 16
TP = 8
NEG_LARGE = -1e30
TOP_FLOOR = -1e29
EPSILON = 1e-05
VMEM_LIMIT = 12 * 1024 * 1024
FLOPS = 10**10

F32 = jnp.float32
BF16 = jnp.bfloat16


def exchange(blocks, axis):
    return lax.all_to_all(blocks, axis, split_axis=0, concat_axis=0, tiled=True)


def permute(value, pairs):
    return lax.ppermute(value, "tp", pairs)


def swap_cores(value):
    return permute(value, [(i, i ^ 1) for i in range(TP)])


def half_here():
    tp = lax.axis_index("tp")
    return (tp + (tp >> 1)) & 1


def along_y(value):
    return [permute(value, [(i, i ^ mask) for i in range(TP)]) for mask in (3, 4, 7)]


def call(kernel, outs, args, scratch=(), flops=0, memory=pltpu.VMEM, limit=VMEM_LIMIT):
    moved = sum(math.prod(a.shape) * a.dtype.itemsize for a in list(args) + list(outs))
    return pl.pallas_call(
        kernel,
        out_shape=tuple(outs),
        in_specs=[pl.BlockSpec(memory_space=memory)] * len(args),
        out_specs=tuple(pl.BlockSpec(memory_space=pltpu.VMEM) for _ in outs),
        scratch_shapes=list(scratch),
        compiler_params=pltpu.CompilerParams(vmem_limit_bytes=limit),
        cost_estimate=pl.CostEstimate(flops=flops, bytes_accessed=moved, transcendentals=0),
    )(*args)


def shaped(shape, dtype=F32):
    return jax.ShapeDtypeStruct(shape, dtype)


def attention_kernel(*refs):
    sources, packed, copies, sems = refs[:7], refs[7], refs[8:15], refs[15]
    len_ref, own_ref, q_ref, kn_ref, vn_ref, k_ref, v_ref = copies
    seqs, slots, dim = k_ref.shape
    news = kn_ref.shape[0]
    drafts = news // seqs
    rows = q_ref.shape[0] // seqs
    small = [pltpu.make_async_copy(sources[i], copies[i], sems.at[i]) for i in range(5)]
    keys = [
        pltpu.make_async_copy(sources[5].at[s], k_ref.at[s], sems.at[5 + s]) for s in range(seqs)
    ]
    values = [
        pltpu.make_async_copy(sources[6].at[s], v_ref.at[s], sems.at[5 + seqs + s])
        for s in range(seqs)
    ]
    for copy in keys + small + values:
        copy.start()
    kvp = lax.axis_index("kvp")
    exponent = math.log2(math.e) / math.sqrt(dim)
    linear = lax.broadcasted_iota(jnp.int32, (1, slots), 1) * KVP + kvp
    new_id = lax.broadcasted_iota(jnp.int32, (rows, news), 1)
    row_draft = lax.broadcasted_iota(jnp.int32, (rows, news), 0) % drafts
    lane = lax.broadcasted_iota(jnp.int32, (rows, dim), 1)
    contract = (((1,), (1,)), ((), ()))
    for copy in small + keys:
        copy.wait()
    stats, weights, fresh_weights = [], [], []
    for s in range(seqs):
        length, owner = len_ref[s], own_ref[s]
        offset = (owner - length) & (KVP - 1)
        position = linear - offset
        live = (position >= 0) & (position < length)
        draft = new_id - drafts * s
        fresh = (draft >= 0) & (draft <= row_draft) & (((owner + draft) & (KVP - 1)) == kvp)
        q = q_ref[rows * s : rows * (s + 1), :]
        fresh_scores = lax.dot_general(q, kn_ref[...], contract, preferred_element_type=F32)
        scores = lax.dot_general(q, k_ref[s], contract, preferred_element_type=F32)
        scores = jnp.where(live, scores, NEG_LARGE)
        fresh_scores = jnp.where(fresh, fresh_scores, NEG_LARGE)
        top = jnp.maximum(
            jnp.max(scores, axis=1, keepdims=True), jnp.max(fresh_scores, axis=1, keepdims=True)
        )
        top = jnp.maximum(top, TOP_FLOOR)
        weight = jnp.exp2((scores - top) * exponent)
        fresh_weight = jnp.exp2((fresh_scores - top) * exponent)
        total = jnp.sum(weight, axis=1, keepdims=True)
        total = total + jnp.sum(fresh_weight, axis=1, keepdims=True)
        weights.append(weight.astype(BF16))
        fresh_weights.append(fresh_weight.astype(BF16))
        at = 2 * (s // 2)
        top = top * exponent
        stats.append(jnp.where(lane == at, top, jnp.where(lane == at + 1, total, 0.0)))
    for copy in values:
        copy.wait()
    for s in range(seqs):
        sums = jnp.dot(weights[s], v_ref[s], preferred_element_type=F32)
        sums = sums + jnp.dot(fresh_weights[s], vn_ref[...], preferred_element_type=F32)
        for h in range(rows // drafts):
            packed[h, drafts * s : drafts * (s + 1), :] = sums[drafts * h : drafts * (h + 1), :]
    for part in range(2):
        both = stats[part] + stats[part + 2]
        base = 16 + drafts * part
        for h in range(rows // drafts):
            packed[h, base : base + drafts, :] = both[drafts * h : drafts * (h + 1), :]


def project(att, w_ref, out_ref, half):
    width = out_ref.shape[-1]
    for k in range(KVP):
        start = pl.multiple_of((2 * k + half) * width, width)
        out_ref[k] = jnp.dot(att, w_ref[:, pl.ds(start, width)], preferred_element_type=F32)


def project_other_kernel(parts, w_ref, att_ref, out_ref):
    halves = []
    for half in range(2):
        tops = parts[:, 16:24, 2 * half : 2 * half + 1]
        totals = parts[:, 16:24, 2 * half + 1 : 2 * half + 2]
        scales = jnp.exp2(tops - jnp.max(tops, axis=0, keepdims=True))
        total = jnp.sum(totals * scales, axis=0)
        sums = jnp.sum(parts[:, 8 * half : 8 * half + 8, :] * scales, axis=0)
        halves.append(sums / total)
    att = jnp.concatenate(halves, axis=0).astype(BF16)
    att_ref[...] = att
    project(att, w_ref, out_ref, 1 - half_here())


def project_own_kernel(att_ref, w_ref, out_ref):
    project(att_ref[...], w_ref, out_ref, half_here())


def add_kernel(a, b, out):
    out[...] = a[...] + b[...]


def sum_kernel(parts, out):
    out[...] = jnp.sum(parts[...], axis=0)


def sum_y_kernel(own, one, two, three, out):
    out[...] = (own[...] + two[...]) + (one[...] + three[...])


def joined(own, got):
    first = half_here() == 0
    mine, theirs = own[...], got[...]
    return jnp.concatenate(
        [jnp.where(first, mine, theirs), jnp.where(first, theirs, mine)], axis=1
    )


def widened(added, res_ref, half):
    width = added.shape[1]
    residual = jnp.concatenate(
        [
            jnp.where(half == 0, rows[:, :width], rows[:, width:])
            for rows in (res_ref[s].astype(F32) for s in range(res_ref.shape[0]))
        ],
        axis=0,
    )
    return (residual + added[...]).astype(BF16).astype(F32)


def scaled(wide, gain_ref, half):
    width = wide.shape[1]
    gain = jnp.where(half == 0, gain_ref[:, :width], gain_ref[:, width:])
    return (wide * gain).astype(BF16)


def half_rows(w_ref, half, columns):
    width = w_ref.shape[0] // 2
    return w_ref[pl.ds(pl.multiple_of(half * width, width), width), columns]


def gate_up_own_kernel(own, res_ref, gain_ref, gate_ref, up_ref, wide_ref, gate_out, up_out):
    half = half_here()
    wide = widened(own, res_ref, half)
    wide_ref[...] = wide
    inputs = scaled(wide, gain_ref, half)
    for column in range(0, gate_ref.shape[1], 256):
        columns = slice(column, column + 256)
        for w_ref, out in ((gate_ref, gate_out), (up_ref, up_out)):
            out[:, columns] = jnp.dot(
                inputs, half_rows(w_ref, half, columns), preferred_element_type=F32
            )


def gate_up_other_kernel(
    got, mine_ref, res_ref, gain_ref, gate_ref, up_ref, gate_own, up_own, wide_ref, out
):
    half = 1 - half_here()
    theirs, mine = widened(got, res_ref, half), mine_ref[...]
    wide_ref[...] = jnp.concatenate(
        [jnp.where(half == 1, mine, theirs), jnp.where(half == 1, theirs, mine)], axis=1
    )
    squares = jnp.sum(mine * mine + theirs * theirs, axis=1, keepdims=True)
    inputs = scaled(theirs, gain_ref, half)
    last = []
    for block in range(13):
        columns = slice(256 * block, 256 * (block + 1))
        for start, w_ref, own in ((0, gate_ref, gate_own), (384, up_ref, up_own)):
            part = own[:, columns] + jnp.dot(
                inputs, half_rows(w_ref, half, columns), preferred_element_type=F32
            )
            if block == 12:
                last.append(part)
                continue
            for side in range(2):
                pair, at = divmod(2 * block + side, 3)
                at = start + 128 * at
                for r in range(2):
                    out[2 * pair + r, :, at : at + 128] = part[
                        8 * r : 8 * r + 8, 128 * side : 128 * (side + 1)
                    ]
    spread = jnp.broadcast_to(squares, (mine.shape[0], 64))
    for pair in range(KVP // 2):
        columns = slice(32 * pair, 32 * (pair + 1))
        mixed = jnp.concatenate([last[0][:, columns], last[1][:, columns], spread], axis=1)
        for r in range(2):
            out[2 * pair + r, :, 768:896] = mixed[8 * r : 8 * r + 8]


def gated(gate, up):
    active = gate / (1.0 + jnp.exp(-gate)) * up
    return active.astype(BF16).astype(F32)


def active_kernel(parts, out):
    total = jnp.sum(parts[...], axis=0)
    mixed = total[:, 768:896]
    factor = lax.rsqrt(mixed[:, 64:65] / D + EPSILON)
    active = gated(total[:, :384] * factor, total[:, 384:768] * factor)
    extra = gated(mixed[:, :32] * factor, mixed[:, 32:64] * factor)
    extra = jnp.concatenate([extra, jnp.zeros((8, 96), F32)], axis=1)
    for i in range(out.shape[0]):
        out[i, :, :384] = active
        out[i, :, 384:] = extra


def down(active, w_ref, out, half):
    width = out.shape[1]
    for column in range(0, width, 256):
        start = pl.multiple_of(half * width + column, 256)
        out[:, column : column + 256] = jnp.dot(
            active, w_ref[:, pl.ds(start, 256)], preferred_element_type=F32
        )


def down_other_kernel(parts, w_ref, active_ref, out):
    halves = []
    for r in range(2):
        pairs = [parts[2 * p + r] for p in range(KVP // 2)]
        columns = [p[:, :384] for p in pairs] + [p[:, 384:416] for p in pairs]
        halves.append(jnp.concatenate(columns, axis=1))
    active = jnp.concatenate(halves, axis=0).astype(BF16)
    active_ref[...] = active
    down(active, w_ref, out, 1 - half_here())


def down_own_kernel(active_ref, w_ref, out):
    down(active_ref[...], w_ref, out, half_here())


def finish_kernel(own, got, wide_ref, att_ref, att_out, mid_out, out):
    lowered = joined(own, got)
    wide = wide_ref[...]
    total = wide + lowered
    att_out[...] = att_ref[...]
    seqs, drafts, _ = out.shape
    for s in range(seqs):
        mid_out[s] = wide[drafts * s : drafts * (s + 1)].astype(BF16)
        out[s] = total[drafts * s : drafts * (s + 1)].astype(BF16)


def body(
    queries,
    key_cache_rows,
    value_cache_rows,
    k_new,
    v_new,
    lengths,
    new_owner,
    residual,
    norm_gain,
    out_weight,
    gate_weight,
    up_weight,
    down_weight,
):
    seqs, heads, drafts, dim = queries.shape
    slots = key_cache_rows.shape[2]
    rows, width = seqs * drafts, residual.shape[-1]
    half = width // 2

    in_hbm = [
        pltpu.with_memory_space_constraint(x, pltpu.HBM)
        for x in (
            lengths,
            new_owner,
            queries.reshape(seqs * heads * drafts, dim),
            k_new.reshape(rows, dim),
            v_new.reshape(rows, dim),
            key_cache_rows.reshape(seqs, slots, dim),
            value_cache_rows.reshape(seqs, slots, dim),
        )
    ]
    (parts,) = call(
        attention_kernel,
        [shaped((KVP, 24, dim))],
        in_hbm,
        scratch=[
            pltpu.SMEM((seqs,), jnp.int32),
            pltpu.SMEM((seqs,), jnp.int32),
            pltpu.VMEM((seqs * heads * drafts, dim), BF16),
            pltpu.VMEM((rows, dim), BF16),
            pltpu.VMEM((rows, dim), BF16),
            pltpu.VMEM((seqs, slots, dim), BF16),
            pltpu.VMEM((seqs, slots, dim), BF16),
            pltpu.SemaphoreType.DMA((5 + 2 * seqs,)),
        ],
        flops=FLOPS,
        memory=pltpu.HBM,
    )
    parts = exchange(parts, "kvp")
    weight = out_weight.reshape(dim, -1)
    chunks = shaped((KVP, rows, half))
    flat_rows, theirs = call(
        project_other_kernel, [shaped((rows, dim), BF16), chunks], [parts, weight], flops=FLOPS
    )
    got = swap_cores(theirs)
    (mine,) = call(project_own_kernel, [chunks], [flat_rows, weight], flops=FLOPS)
    (parts,) = call(add_kernel, [chunks], [mine, got], flops=FLOPS)
    (part,) = call(sum_kernel, [shaped((rows, half))], [exchange(parts, "kvp")], flops=FLOPS)
    piece, full = shaped((rows, half)), shaped((rows, width))
    (part,) = call(sum_y_kernel, [piece], [part, *along_y(part)], flops=FLOPS)
    got = swap_cores(part)
    gain, hidden = norm_gain.reshape(1, width), shaped((rows, gate_weight.shape[1]))
    mine, gate_own, up_own = call(
        gate_up_own_kernel,
        [piece, hidden, hidden],
        [part, residual, gain, gate_weight, up_weight],
        flops=FLOPS,
    )
    wide, parts = call(
        gate_up_other_kernel,
        [full, shaped((KVP, 8, 896))],
        [got, mine, residual, gain, gate_weight, up_weight, gate_own, up_own],
        flops=FLOPS,
    )
    (parts,) = call(
        active_kernel, [shaped((KVP, 8, 512))], [exchange(parts, "kvp")], flops=FLOPS
    )
    active, theirs = call(
        down_other_kernel,
        [shaped((rows, down_weight.shape[0]), BF16), piece],
        [exchange(parts, "kvp"), down_weight],
        flops=FLOPS,
    )
    got = swap_cores(theirs)
    (lowered,) = call(down_own_kernel, [piece], [active, down_weight], flops=FLOPS)
    (lowered,) = call(add_kernel, [piece], [lowered, got])
    (lowered,) = call(sum_y_kernel, [piece], [lowered, *along_y(lowered)])
    attended, stream_mid, layer_out = call(
        finish_kernel,
        [
            shaped((rows, dim), BF16),
            shaped((seqs, drafts, width), BF16),
            shaped((seqs, drafts, width), BF16),
        ],
        [lowered, swap_cores(lowered), wide, flat_rows],
    )
    return attended.reshape(seqs, 1, 1, drafts, dim), stream_mid, layer_out


def solution(mesh):
    placed = (
        P(None, "tp", None, None),
        P(None, "tp", "kvp", None),
        P(None, "tp", "kvp", None),
        P(None, "tp", None, None),
        P(None, "tp", None, None),
        P(),
        P(),
        P(None, None, "kvp"),
        P("kvp"),
        P("tp", "kvp", None, None),
        P("kvp", "tp"),
        P("kvp", "tp"),
        P("tp", "kvp"),
    )
    return jax.shard_map(
        body,
        mesh=mesh,
        in_specs=placed,
        out_specs=(P(None, "tp", "kvp", None, None), P(None, None, "kvp"), P(None, None, "kvp")),
        check_vma=False,
    )
```

```python
import math

import jax
import jax.numpy as jnp
from jax import lax
from jax.experimental import pallas as pl
from jax.experimental.pallas import tpu as pltpu
from jax.sharding import PartitionSpec as P

D = 16384
KVP = 16
TP = 8
NEG_LARGE = -1e30
TOP_FLOOR = -1e29
EPSILON = 1e-05
VMEM_LIMIT = 12 * 1024 * 1024
FLOPS = 10**10

F32 = jnp.float32
BF16 = jnp.bfloat16


def exchange(blocks, axis):
    return lax.all_to_all(blocks, axis, split_axis=0, concat_axis=0, tiled=True)


def permute(value, pairs):
    return lax.ppermute(value, "tp", pairs)


def swap_cores(value):
    return permute(value, [(i, i ^ 1) for i in range(TP)])


def half_here():
    tp = lax.axis_index("tp")
    return (tp + (tp >> 1)) & 1


def along_y(value):
    return [permute(value, [(i, i ^ mask) for i in range(TP)]) for mask in (3, 4, 7)]


def call(kernel, outs, args, scratch=(), flops=0, memory=pltpu.VMEM, limit=VMEM_LIMIT):
    moved = sum(math.prod(a.shape) * a.dtype.itemsize for a in list(args) + list(outs))
    return pl.pallas_call(
        kernel,
        out_shape=tuple(outs),
        in_specs=[pl.BlockSpec(memory_space=memory)] * len(args),
        out_specs=tuple(pl.BlockSpec(memory_space=pltpu.VMEM) for _ in outs),
        scratch_shapes=list(scratch),
        compiler_params=pltpu.CompilerParams(vmem_limit_bytes=limit),
        cost_estimate=pl.CostEstimate(flops=flops, bytes_accessed=moved, transcendentals=0),
    )(*args)


def shaped(shape, dtype=F32):
    return jax.ShapeDtypeStruct(shape, dtype)


def attention_kernel(*refs):
    sources, packed, copies, sems = refs[:7], refs[7], refs[8:15], refs[15]
    len_ref, own_ref, q_ref, kn_ref, vn_ref, k_ref, v_ref = copies
    seqs, slots, dim = k_ref.shape
    news = kn_ref.shape[0]
    drafts = news // seqs
    rows = q_ref.shape[0] // seqs
    small = [pltpu.make_async_copy(sources[i], copies[i], sems.at[i]) for i in range(5)]
    keys = [
        pltpu.make_async_copy(sources[5].at[s], k_ref.at[s], sems.at[5 + s]) for s in range(seqs)
    ]
    values = [
        pltpu.make_async_copy(sources[6].at[s], v_ref.at[s], sems.at[5 + seqs + s])
        for s in range(seqs)
    ]
    for copy in keys + small + values:
        copy.start()
    kvp = lax.axis_index("kvp")
    exponent = math.log2(math.e) / math.sqrt(dim)
    linear = lax.broadcasted_iota(jnp.int32, (1, slots), 1) * KVP + kvp
    new_id = lax.broadcasted_iota(jnp.int32, (rows, news), 1)
    row_draft = lax.broadcasted_iota(jnp.int32, (rows, news), 0) % drafts
    lane = lax.broadcasted_iota(jnp.int32, (rows, dim), 1)
    contract = (((1,), (1,)), ((), ()))
    for copy in small + keys:
        copy.wait()
    stats, weights, fresh_weights = jnp.zeros((rows, dim), F32), [], []
    for s in range(seqs):
        length, owner = len_ref[s], own_ref[s]
        offset = (owner - length) & (KVP - 1)
        position = linear - offset
        live = (position >= 0) & (position < length)
        draft = new_id - drafts * s
        fresh = (draft >= 0) & (draft <= row_draft) & (((owner + draft) & (KVP - 1)) == kvp)
        q = q_ref[rows * s : rows * (s + 1), :]
        fresh_scores = lax.dot_general(q, kn_ref[...], contract, preferred_element_type=F32)
        scores = lax.dot_general(q, k_ref[s], contract, preferred_element_type=F32)
        scores = jnp.where(live, scores, NEG_LARGE)
        fresh_scores = jnp.where(fresh, fresh_scores, NEG_LARGE)
        top = jnp.maximum(
            jnp.max(scores, axis=1, keepdims=True), jnp.max(fresh_scores, axis=1, keepdims=True)
        )
        top = jnp.maximum(top, TOP_FLOOR)
        weight = jnp.exp2((scores - top) * exponent)
        fresh_weight = jnp.exp2((fresh_scores - top) * exponent)
        total = jnp.sum(weight, axis=1, keepdims=True)
        total = total + jnp.sum(fresh_weight, axis=1, keepdims=True)
        weights.append(weight.astype(BF16))
        fresh_weights.append(fresh_weight.astype(BF16))
        stats = jnp.where(lane == 2 * s, top * exponent, stats)
        stats = jnp.where(lane == 2 * s + 1, total, stats)
    for copy in values:
        copy.wait()
    for s in range(seqs):
        sums = jnp.dot(weights[s], v_ref[s], preferred_element_type=F32)
        sums = sums + jnp.dot(fresh_weights[s], vn_ref[...], preferred_element_type=F32)
        for h in range(rows // drafts):
            packed[h, s] = sums[drafts * h : drafts * (h + 1), :]
    for h in range(rows // drafts):
        packed[h, seqs] = stats[drafts * h : drafts * (h + 1), :]


def project(att, w_ref, out_ref, half):
    width = out_ref.shape[-1]
    for k in range(KVP):
        start = pl.multiple_of((2 * k + half) * width, width)
        out_ref[k] = jnp.dot(att, w_ref[:, pl.ds(start, width)], preferred_element_type=F32)


def project_other_kernel(parts, w_ref, att_ref, out_ref):
    pieces = []
    seqs = parts.shape[1] - 1
    for s in range(seqs):
        tops = parts[:, seqs, :, 2 * s : 2 * s + 1]
        totals = parts[:, seqs, :, 2 * s + 1 : 2 * s + 2]
        scales = jnp.exp2(tops - jnp.max(tops, axis=0, keepdims=True))
        total = jnp.sum(totals * scales, axis=0)
        pieces.append(jnp.sum(parts[:, s] * scales, axis=0) / total)
    att = jnp.concatenate(pieces, axis=0).astype(BF16)
    att_ref[...] = att
    project(att, w_ref, out_ref, 1 - half_here())


def project_own_kernel(att_ref, w_ref, out_ref):
    project(att_ref[...], w_ref, out_ref, half_here())


def add_kernel(a, b, out):
    out[...] = a[...] + b[...]


def sum_kernel(parts, out):
    out[...] = jnp.sum(parts[...], axis=0)


def sum_y_kernel(own, one, two, three, out):
    out[...] = (own[...] + two[...]) + (one[...] + three[...])


def joined(own, got):
    first = half_here() == 0
    mine, theirs = own[...], got[...]
    return jnp.concatenate(
        [jnp.where(first, mine, theirs), jnp.where(first, theirs, mine)], axis=1
    )


def widened(added, res_ref, half):
    width = added.shape[1]
    residual = jnp.concatenate(
        [
            jnp.where(half == 0, rows[:, :width], rows[:, width:])
            for rows in (res_ref[s].astype(F32) for s in range(res_ref.shape[0]))
        ],
        axis=0,
    )
    return (residual + added[...]).astype(BF16).astype(F32)


def scaled(wide, gain_ref, half):
    width = wide.shape[1]
    gain = jnp.where(half == 0, gain_ref[:, :width], gain_ref[:, width:])
    return (wide * gain).astype(BF16)


def half_rows(w_ref, half, columns):
    width = w_ref.shape[0] // 2
    return w_ref[pl.ds(pl.multiple_of(half * width, width), width), columns]


def gate_up_own_kernel(own, res_ref, gain_ref, gate_ref, up_ref, wide_ref, gate_out, up_out):
    half = half_here()
    wide = widened(own, res_ref, half)
    wide_ref[...] = wide
    inputs = scaled(wide, gain_ref, half)
    for column in range(0, gate_ref.shape[1], 256):
        columns = slice(column, column + 256)
        for w_ref, out in ((gate_ref, gate_out), (up_ref, up_out)):
            out[:, columns] = jnp.dot(
                inputs, half_rows(w_ref, half, columns), preferred_element_type=F32
            )


def gate_up_other_kernel(
    got, mine_ref, res_ref, gain_ref, gate_ref, up_ref, gate_own, up_own, wide_ref, out
):
    half = 1 - half_here()
    theirs, mine = widened(got, res_ref, half), mine_ref[...]
    wide_ref[...] = jnp.concatenate(
        [jnp.where(half == 1, mine, theirs), jnp.where(half == 1, theirs, mine)], axis=1
    )
    squares = jnp.sum(mine * mine + theirs * theirs, axis=1, keepdims=True)
    inputs = scaled(theirs, gain_ref, half)
    last = []
    for block in range(13):
        columns = slice(256 * block, 256 * (block + 1))
        for start, w_ref, own in ((0, gate_ref, gate_own), (384, up_ref, up_own)):
            part = own[:, columns] + jnp.dot(
                inputs, half_rows(w_ref, half, columns), preferred_element_type=F32
            )
            if block == 12:
                last.append(part)
                continue
            for side in range(2):
                pair, at = divmod(2 * block + side, 3)
                at = start + 128 * at
                for r in range(2):
                    out[2 * pair + r, :, at : at + 128] = part[
                        8 * r : 8 * r + 8, 128 * side : 128 * (side + 1)
                    ]
    spread = jnp.broadcast_to(squares, (mine.shape[0], 64))
    for pair in range(KVP // 2):
        columns = slice(32 * pair, 32 * (pair + 1))
        mixed = jnp.concatenate([last[0][:, columns], last[1][:, columns], spread], axis=1)
        for r in range(2):
            out[2 * pair + r, :, 768:896] = mixed[8 * r : 8 * r + 8]


def gated(gate, up):
    active = gate / (1.0 + jnp.exp(-gate)) * up
    return active.astype(BF16).astype(F32)


def active_kernel(parts, out):
    total = jnp.sum(parts[...], axis=0)
    mixed = total[:, 768:896]
    factor = lax.rsqrt(mixed[:, 64:65] / D + EPSILON)
    active = gated(total[:, :384] * factor, total[:, 384:768] * factor)
    extra = gated(mixed[:, :32] * factor, mixed[:, 32:64] * factor)
    extra = jnp.concatenate([extra[:4], extra[4:], jnp.zeros((4, 64), F32)], axis=1)
    for i in range(out.shape[0]):
        for block in range(3):
            columns = slice(128 * block, 128 * (block + 1))
            out[i, 2 * block] = active[:4, columns]
            out[i, 2 * block + 1] = active[4:, columns]
        out[i, 6] = extra


def down(active, w_ref, out, half):
    width = out.shape[1]
    for column in range(0, width, 256):
        start = pl.multiple_of(half * width + column, 256)
        out[:, column : column + 256] = jnp.dot(
            active, w_ref[:, pl.ds(start, 256)], preferred_element_type=F32
        )


def down_other_kernel(parts, w_ref, active_ref, out):
    halves = []
    for r in range(2):
        columns, extras = [], []
        for member in range(r, KVP, 2):
            for block in range(3):
                rows = [parts[member, 2 * block], parts[member, 2 * block + 1]]
                columns.append(jnp.concatenate(rows, axis=0))
            last = parts[member, 6]
            extras.append(jnp.concatenate([last[:, :32], last[:, 32:64]], axis=0))
        halves.append(jnp.concatenate(columns + extras, axis=1))
    active = jnp.concatenate(halves, axis=0).astype(BF16)
    active_ref[...] = active
    down(active, w_ref, out, 1 - half_here())


def down_own_kernel(active_ref, w_ref, out):
    down(active_ref[...], w_ref, out, half_here())


def finish_kernel(own, got, wide_ref, att_ref, att_out, mid_out, out):
    lowered = joined(own, got)
    wide = wide_ref[...]
    total = wide + lowered
    att_out[...] = att_ref[...]
    seqs, drafts, _ = out.shape
    for s in range(seqs):
        mid_out[s] = wide[drafts * s : drafts * (s + 1)].astype(BF16)
        out[s] = total[drafts * s : drafts * (s + 1)].astype(BF16)


def body(
    queries,
    key_cache_rows,
    value_cache_rows,
    k_new,
    v_new,
    lengths,
    new_owner,
    residual,
    norm_gain,
    out_weight,
    gate_weight,
    up_weight,
    down_weight,
):
    seqs, heads, drafts, dim = queries.shape
    slots = key_cache_rows.shape[2]
    rows, width = seqs * drafts, residual.shape[-1]
    half = width // 2

    in_hbm = [
        pltpu.with_memory_space_constraint(x, pltpu.HBM)
        for x in (
            lengths,
            new_owner,
            queries.reshape(seqs * heads * drafts, dim),
            k_new.reshape(rows, dim),
            v_new.reshape(rows, dim),
            key_cache_rows.reshape(seqs, slots, dim),
            value_cache_rows.reshape(seqs, slots, dim),
        )
    ]
    (parts,) = call(
        attention_kernel,
        [shaped((KVP, seqs + 1, drafts, dim))],
        in_hbm,
        scratch=[
            pltpu.SMEM((seqs,), jnp.int32),
            pltpu.SMEM((seqs,), jnp.int32),
            pltpu.VMEM((seqs * heads * drafts, dim), BF16),
            pltpu.VMEM((rows, dim), BF16),
            pltpu.VMEM((rows, dim), BF16),
            pltpu.VMEM((seqs, slots, dim), BF16),
            pltpu.VMEM((seqs, slots, dim), BF16),
            pltpu.SemaphoreType.DMA((5 + 2 * seqs,)),
        ],
        flops=FLOPS,
        memory=pltpu.HBM,
    )
    parts = exchange(parts, "kvp")
    weight = out_weight.reshape(dim, -1)
    chunks = shaped((KVP, rows, half))
    flat_rows, theirs = call(
        project_other_kernel, [shaped((rows, dim), BF16), chunks], [parts, weight], flops=FLOPS
    )
    got = swap_cores(theirs)
    (mine,) = call(project_own_kernel, [chunks], [flat_rows, weight], flops=FLOPS)
    (parts,) = call(add_kernel, [chunks], [mine, got], flops=FLOPS)
    (part,) = call(sum_kernel, [shaped((rows, half))], [exchange(parts, "kvp")], flops=FLOPS)
    piece, full = shaped((rows, half)), shaped((rows, width))
    (part,) = call(sum_y_kernel, [piece], [part, *along_y(part)], flops=FLOPS)
    got = swap_cores(part)
    gain, hidden = norm_gain.reshape(1, width), shaped((rows, gate_weight.shape[1]))
    mine, gate_own, up_own = call(
        gate_up_own_kernel,
        [piece, hidden, hidden],
        [part, residual, gain, gate_weight, up_weight],
        flops=FLOPS,
    )
    wide, parts = call(
        gate_up_other_kernel,
        [full, shaped((KVP, 8, 896))],
        [got, mine, residual, gain, gate_weight, up_weight, gate_own, up_own],
        flops=FLOPS,
    )
    (parts,) = call(
        active_kernel, [shaped((KVP, 7, 4, 128))], [exchange(parts, "kvp")], flops=FLOPS
    )
    active, theirs = call(
        down_other_kernel,
        [shaped((rows, down_weight.shape[0]), BF16), piece],
        [exchange(parts, "kvp"), down_weight],
        flops=FLOPS,
    )
    got = swap_cores(theirs)
    (lowered,) = call(down_own_kernel, [piece], [active, down_weight], flops=FLOPS)
    (lowered,) = call(add_kernel, [piece], [lowered, got])
    (lowered,) = call(sum_y_kernel, [piece], [lowered, *along_y(lowered)])
    attended, stream_mid, layer_out = call(
        finish_kernel,
        [
            shaped((rows, dim), BF16),
            shaped((seqs, drafts, width), BF16),
            shaped((seqs, drafts, width), BF16),
        ],
        [lowered, swap_cores(lowered), wide, flat_rows],
    )
    return attended.reshape(seqs, 1, 1, drafts, dim), stream_mid, layer_out


def solution(mesh):
    placed = (
        P(None, "tp", None, None),
        P(None, "tp", "kvp", None),
        P(None, "tp", "kvp", None),
        P(None, "tp", None, None),
        P(None, "tp", None, None),
        P(),
        P(),
        P(None, None, "kvp"),
        P("kvp"),
        P("tp", "kvp", None, None),
        P("kvp", "tp"),
        P("kvp", "tp"),
        P("tp", "kvp"),
    )
    return jax.shard_map(
        body,
        mesh=mesh,
        in_specs=placed,
        out_specs=(P(None, "tp", "kvp", None, None), P(None, None, "kvp"), P(None, None, "kvp")),
        check_vma=False,
    )
```
